256 devices in a mesh: chain: 32 (over y_hi, z, core), mp: 8 (over y_lo, x).
Axes of the slice: x: 4, y: 4 (y_hi: 2, y_lo: 2; y = y_hi * 2 + y_lo), z: 8, core: 2. Of those that a mesh axis runs over, the one named last changes fastest.
Arguments:
- latents: float32 [1, 128, 4, 40, 64], P(None, 'chain', None, 'mp'), may hold values from -6 to 6
- step_noise: float32 [1, 128, 4, 40, 64], P(None, 'chain', None, 'mp'), may hold values from -6 to 6
- fresh_noise: float32 [1, 4, 40, 64], P(None, None, 'mp'), may hold values from -6 to 6
- timesteps: int32 [128], P('chain'), may hold values from 0 to 999
- step_coefs: float32 [3, 128], P(None, 'chain'), may hold values from -0.7 to 1.15
- inlet_weight: bfloat16 [9, 4, 320], replicated, may hold values from -1 to 1
- time_first: bfloat16 [320, 1280], replicated, may hold values from -0.3125 to 0.3125
- time_second: bfloat16 [1280, 320], replicated, may hold values from -0.15625 to 0.15625
- res_weight: bfloat16 [9, 320, 320], replicated, may hold values from -0.109375 to 0.109375
- query_weight: bfloat16 [320, 320], replicated, may hold values from -1.35 to 1.35
- key_weight: bfloat16 [320, 320], replicated, may hold values from -1.35 to 1.35
- value_weight: bfloat16 [320, 320], replicated, may hold values from -0.3125 to 0.3125
- output_weight: bfloat16 [320, 320], replicated, may hold values from -0.3125 to 0.3125
- outlet_weight: bfloat16 [9, 320, 4], replicated, may hold values from -0.109375 to 0.109375
Outputs:
- stepped: float32 [1, 128, 4, 40, 64], P(None, 'chain', None, 'mp')
- advanced: float32 [1, 128, 4, 40, 64], P(None, 'chain', None, 'mp')
The draws below stay inside these ranges and needn't reach their ends.
All inputs are finite; a program needn't handle non-finite values.
Results may differ from the reference program's by a relative error of at most 0.0029.
Values may be sent and summed in bfloat16 or wider, within the bound.
No kernel may reach another device: no remote copies, remote signals or barrier semaphores. Data moves between devices by JAX's collectives and lax.ppermute only.
A program may use at most 128 MiB of HBM per device.

```python
import math
import jax
import jax.numpy as jnp
from jax import lax

HEADS = 5
HEAD_DIM = 64
TEMB = 1280
LAT = 4
LAT_H = 40
LAT_W = 64
WINDOW = 16
PROMPTS = 1
C = 320
QUEUE = 128


def draw_query_weight(key, part):
    own_part = jax.random.truncated_normal(jax.random.fold_in(key, 11), -3.0, 3.0, (C, C), jnp.float32) / max(math.sqrt(C), 16.0)
    return own_part.astype(jnp.bfloat16)


def draw_key_weight(key, part):
    own_part = jax.random.truncated_normal(jax.random.fold_in(key, 13), -3.0, 3.0, (C, C), jnp.float32) / max(math.sqrt(C), 16.0)
    return own_part.astype(jnp.bfloat16)


def draw_step_coefs(key, part):
    uniform_part = jax.random.uniform(key, (3, QUEUE), jnp.float32)
    lowest = jnp.array([0.85, -0.7, 0.1], jnp.float32)
    highest = jnp.array([1.15, -0.2, 0.4], jnp.float32)
    return lowest[:, None] + (highest - lowest)[:, None] * uniform_part


def plant(values, rng, least, top_value):
    shape = values.shape
    spot = [jax.random.randint(jax.random.fold_in(rng, axis), (), 0, shape[axis]) for axis in range(len(shape))]
    values = values.at[tuple(spot)].set(least)
    longest = shape.index(max(shape))
    spot[longest] = (spot[longest] + 1) % shape[longest]
    return values.at[tuple(spot)].set(top_value)


def block_scale(stream_key, dims, pieces, low, high):
    factor_of, own = 1.0, jax.random.fold_in(stream_key, 6)
    for dim, blocks in pieces:
        steps = jnp.exp(jax.random.uniform(jax.random.fold_in(own, dim), (blocks,), jnp.float32, low / len(pieces), high / len(pieces)))
        factor_of = factor_of * jnp.repeat(steps, dims[dim] // blocks).reshape([-1 if axis == dim else 1 for axis in range(len(dims))])
    return factor_of


def normal_values(rng, shape, deviation, most, cuts=(), kind=jnp.bfloat16):
    loudness = block_scale(rng, shape, cuts, -0.22, 0.18) if cuts else 1.0
    drawn = jax.random.normal(rng, shape, jnp.float32) * deviation * loudness
    return jnp.minimum(jnp.maximum(drawn, -most), most).astype(kind)


def setup_inputs(seed: int = 0) -> dict:
    key_of = jax.random.split(jax.random.key(seed), 15)
    return {
        "latents": normal_values(key_of[0], (PROMPTS, QUEUE, LAT, LAT_H, LAT_W), 1.0, 6.0, ((1, 32), (3, 8)), jnp.float32),
        "step_noise": normal_values(key_of[1], (PROMPTS, QUEUE, LAT, LAT_H, LAT_W), 1.0, 6.0, ((1, 32), (3, 8)), jnp.float32),
        "fresh_noise": normal_values(key_of[2], (PROMPTS, LAT, LAT_H, LAT_W), 1.0, 6.0, ((2, 8),), jnp.float32),
        "timesteps": plant(jax.random.randint(key_of[3], (QUEUE,), 0, 1000), jax.random.fold_in(key_of[3], 1), 0, 999).astype(jnp.int32),
        "step_coefs": draw_step_coefs(jax.random.fold_in(key_of[14], 71), 0),
        "inlet_weight": normal_values(key_of[5], (9, LAT, C), (9 * LAT) ** -0.5, 1.0),
        "time_first": normal_values(key_of[6], (C, TEMB), C ** -0.5, 0.3125),
        "time_second": normal_values(key_of[7], (TEMB, C), TEMB ** -0.5, 0.15625),
        "res_weight": normal_values(key_of[8], (9, C, C), (9 * C) ** -0.5, 0.109375),
        "query_weight": draw_query_weight(jax.random.fold_in(key_of[14], 71), 0),
        "key_weight": draw_key_weight(jax.random.fold_in(key_of[14], 71), 0),
        "value_weight": normal_values(key_of[11], (C, C), C ** -0.5, 0.3125),
        "output_weight": normal_values(key_of[12], (C, C), C ** -0.5, 0.3125),
        "outlet_weight": normal_values(key_of[13], (9, C, LAT), (9 * C) ** -0.5, 0.109375),
    }


def embed_steps(timesteps):
    half_dim = C // 2
    frequency = jnp.exp(-math.log(10000.0) * jnp.arange(half_dim, dtype=jnp.float32) / half_dim)
    angles = timesteps.astype(jnp.float32)[:, None] * frequency[None, :]
    return jnp.concatenate([jnp.cos(angles), jnp.sin(angles)], axis=1)

def rms_normed(hidden):
    return hidden * lax.rsqrt(lax.optimization_barrier(jnp.mean(hidden * hidden, axis=-1, keepdims=True)) + 1e-05)

def conv_frame(field, weight):
    height = field.shape[0]
    lane_count = field.shape[1]
    padded = jnp.pad(field, ((1, 1), (1, 1), (0, 0)))
    summed = jnp.zeros((height, lane_count, weight.shape[2]), jnp.float32)
    for tap_index in range(9):
        tap_row = tap_index // 3
        tap_col = tap_index % 3
        window = padded[tap_row:tap_row + height, tap_col:tap_col + lane_count, :]
        summed = summed + jnp.einsum('hwc,cd->hwd', window.astype(jnp.float32), weight[tap_index].astype(jnp.float32))
    return summed

def window_attention(queries, key_part, value_part):
    queue_len = queries.shape[0]
    lane_count = queries.shape[1]
    blocks = queue_len // WINDOW
    shaped = (blocks, WINDOW, lane_count, HEADS, HEAD_DIM)
    query_heads = queries.astype(jnp.float32).reshape(shaped)
    key_heads = key_part.astype(jnp.float32).reshape(shaped)
    value_heads = value_part.astype(jnp.float32).reshape(shaped)
    scores = jnp.einsum('nfwhd,ngwhd->nfwhg', query_heads, key_heads) / math.sqrt(HEAD_DIM)
    highest = lax.optimization_barrier(jnp.max(scores, axis=-1, keepdims=True))
    expsum = jnp.exp(scores - highest)
    probs = (expsum / lax.optimization_barrier(jnp.sum(expsum, axis=-1, keepdims=True))).astype(jnp.bfloat16)
    summed = jnp.einsum('nfwhg,ngwhd->nfwhd', probs.astype(jnp.float32), value_heads)
    return summed.reshape(queue_len, lane_count, C).astype(jnp.bfloat16)

def reference(latents, step_noise, fresh_noise, timesteps, step_coefs, inlet_weight, time_first, time_second, res_weight, query_weight, key_weight, value_weight, output_weight, outlet_weight):
    embedded = embed_steps(timesteps).astype(jnp.bfloat16)
    time_hidden = jax.nn.silu(jnp.dot(embedded, time_first, preferred_element_type=jnp.float32)).astype(jnp.bfloat16)
    time_shift = jnp.dot(time_hidden, time_second, preferred_element_type=jnp.float32)

    def front(items_pair):
        frame_latent, frame_shift = items_pair
        latent_in = jnp.transpose(frame_latent, (1, 2, 0)).astype(jnp.bfloat16)
        opening = conv_frame(latent_in, inlet_weight)
        activated = jax.nn.silu(rms_normed(opening) + frame_shift).astype(jnp.bfloat16)
        residual = opening + conv_frame(activated, res_weight)
        normed = rms_normed(residual).astype(jnp.bfloat16).reshape(LAT_H * LAT_W, C)
        queries = jnp.dot(normed, query_weight, preferred_element_type=jnp.float32).astype(jnp.bfloat16)
        key_part = jnp.dot(normed, key_weight, preferred_element_type=jnp.float32).astype(jnp.bfloat16)
        value_part = jnp.dot(normed, value_weight, preferred_element_type=jnp.float32).astype(jnp.bfloat16)
        shaped = (LAT_H, LAT_W, C)
        return (residual, queries.reshape(shaped), key_part.reshape(shaped), value_part.reshape(shaped))

    def one_prompt(items_pair):
        prompt_latent, prompt_noise = items_pair
        residual, queries, key_part, value_part = lax.map(front, (prompt_latent, time_shift))
        by_rows = (jnp.transpose(queries, (1, 0, 2, 3)), jnp.transpose(key_part, (1, 0, 2, 3)), jnp.transpose(value_part, (1, 0, 2, 3)))
        attended = lax.map(lambda triple: window_attention(triple[0], triple[1], triple[2]), by_rows)
        attended = jnp.transpose(attended, (1, 0, 2, 3))

        def back(items):
            frame_resid, frame_att, frame_latent, frame_noise, frame_coef = items
            mixture = frame_resid + jnp.dot(frame_att.reshape(LAT_H * LAT_W, C), output_weight, preferred_element_type=jnp.float32).reshape(LAT_H, LAT_W, C)
            pre_out = jax.nn.silu(rms_normed(mixture)).astype(jnp.bfloat16)
            predicted = jnp.transpose(conv_frame(pre_out, outlet_weight), (2, 0, 1))
            return frame_coef[0] * frame_latent + frame_coef[1] * predicted + frame_coef[2] * frame_noise
        return lax.map(back, (residual, attended, prompt_latent, prompt_noise, jnp.transpose(step_coefs)))
    stepped = lax.map(one_prompt, (latents, step_noise))
    advanced = jnp.concatenate([stepped[:, 1:], fresh_noise[:, None]], axis=1)
    return (stepped, advanced)
```

```python
import functools
import math

import jax
import jax.numpy as jnp
from jax import lax
from jax.experimental import pallas as pl
from jax.experimental.pallas import tpu as pltpu
from jax.sharding import PartitionSpec as P

F32 = jnp.float32
BF16 = jnp.bfloat16
HEADS = 5
HEAD_DIM = 64
C = 320
GROUP = 4


def from_partner(block, bits):
    count = lax.axis_size("chain")
    return lax.ppermute(block, "chain", [(i, i ^ bits) for i in range(count)])


def from_row(block, by):
    count = lax.axis_size("mp")
    pairs = [(i, i + by) for i in range(count) if 0 <= i + by < count]
    return lax.ppermute(block, "mp", pairs)


def embed_steps(timesteps):
    half_dim = C // 2
    frequency = jnp.exp(-math.log(10000.0) * jnp.arange(half_dim, dtype=F32) / half_dim)
    angles = timesteps.astype(F32)[:, None] * frequency[None, :]
    return jnp.concatenate([jnp.cos(angles), jnp.sin(angles)], axis=1)


def halved_silu(half):
    return half * jnp.tanh(half) + half


def inv_rms(values):
    return lax.rsqrt(jnp.sum(values * values, axis=0, keepdims=True) * (1.0 / C) + 1e-05)


def iota(shape, dim):
    return lax.broadcasted_iota(jnp.int32, shape, dim)


def core_kernel(
    s0, s1, s2, s3, win, wres, wqkv, wo, wout, o0, o1, o2, o3, act, opn, accs
):
    tile = lax.axis_index("chain") % GROUP
    row_block = lax.axis_index("mp")
    slabs = [s0[...], s1[...], s2[...], s3[...]]
    shift_rows = jnp.concatenate([s[80:112] for s in slabs], axis=0)
    er, el = iota((128, 640), 0), iota((128, 640), 1)
    pick = (er % 32 // 4 == el // 128) & (er // 32 * 4 + er % 4 == el % 128 // 8)
    spread = lax.dot_general(
        shift_rows.astype(F32).T.astype(BF16),
        pick.astype(F32).astype(BF16),
        (((1,), (0,)), ((), ())),
        preferred_element_type=F32,
    )
    spread = spread[:64] + spread[64:]
    shift = jnp.concatenate([spread[:, 128 * i : 128 * i + 128] for i in range(5)], axis=0) * 0.5
    latent = jnp.concatenate([s[:80] for s in slabs], axis=0)
    lane = iota((128, 384), 1)
    cell, slot, block = lane % 8, lane % 128 // 8, lane // 128
    at = jnp.where(
        block < 2,
        16 * tile + 8 * block + cell,
        jnp.where(cell == 0, 16 * tile - 1, jnp.where(cell == 7, 16 * tile + 16, -1000)),
    )
    src = iota((128, 384), 0)
    same_half = src // 64 == slot % 2
    pair_of = iota((1, 1, 384), 2) % 128 // 16
    pair_no = iota((8, 1, 384), 0)
    columns = []
    for dx in range(3):
        chosen = same_half & (src % 64 == at + (dx - 1))
        moved = jnp.dot(latent, chosen.astype(F32).astype(BF16), preferred_element_type=F32)
        moved = jnp.where(pair_of == pair_no, moved.reshape(8, 40, 384), 0.0)
        columns.append(jnp.sum(moved, axis=0))
    columns.append(jnp.zeros((8, 384), F32))
    columns = jnp.concatenate(columns, axis=0).astype(BF16)
    lane1 = iota((1, 128), 1)
    cell1 = lane1 % 8
    first, last = cell1 == 0, cell1 == 7
    side = jnp.where(
        first & (tile > 0), 1.0, jnp.where(last & (tile < GROUP - 1), 1.0, 0.0)
    )
    rows = lax.axis_size("mp")
    win_f = win[...].astype(F32)
    for r in range(7):
        weight = win_f if r == 0 else pltpu.roll(win_f, r, 1)
        opening = jnp.dot(weight.astype(BF16), columns, preferred_element_type=F32)
        if 1 <= r <= 5:
            opn[r - 1] = opening[:, :256]
        scale = inv_rms(opening) * 0.5
        parts = []
        for t in range(3):
            piece = slice(128 * t, 128 * t + 128)
            part = halved_silu(opening[:, piece] * scale[:, piece] + shift)
            if t == 2:
                part = part * side
            if r == 0:
                part = part * jnp.where(row_block > 0, 1.0, 0.0)
            if r == 6:
                part = part * jnp.where(row_block < rows - 1, 1.0, 0.0)
            parts.append(part)
        a0, a1, edge = parts
        base = 960 * r
        act[base : base + 320, :128] = jnp.where(first, edge, pltpu.roll(a0, 1, 1)).astype(BF16)
        act[base : base + 320, 128:] = jnp.where(
            first, pltpu.roll(a0, 121, 1), pltpu.roll(a1, 1, 1)
        ).astype(BF16)
        act[base + 320 : base + 640, :128] = a0.astype(BF16)
        act[base + 320 : base + 640, 128:] = a1.astype(BF16)
        act[base + 640 : base + 960, :128] = jnp.where(
            last, pltpu.roll(a1, 7, 1), pltpu.roll(a0, 127, 1)
        ).astype(BF16)
        act[base + 640 : base + 960, 128:] = jnp.where(
            last, edge, pltpu.roll(a1, 127, 1)
        ).astype(BF16)
    accs[...] = jnp.zeros_like(accs)
    same_cell = iota((8, 128), 0) == iota((8, 128), 1) % 8
    log2e8 = math.log2(math.e) / math.sqrt(HEAD_DIM)
    for r in range(5):
        residual = opn[r] + jnp.dot(
            wres[...], act[960 * r : 960 * r + 2880, :], preferred_element_type=F32
        )
        normed = (residual * inv_rms(residual)).astype(BF16)
        qkv = jnp.dot(wqkv[...], normed, preferred_element_type=F32).astype(BF16)
        blocks = []
        for b in range(2):
            piece = slice(128 * b, 128 * b + 128)
            heads = []
            for h in range(HEADS):
                query = qkv[64 * h : 64 * h + 64, piece]
                key = qkv[320 + 64 * h : 384 + 64 * h, piece]
                value = qkv[640 + 64 * h : 704 + 64 * h, piece]
                scores = lax.dot_general(
                    key, query, (((0,), (0,)), ((), ())), preferred_element_type=F32
                ).reshape(16, 8, 128)
                highest = jnp.max(scores, axis=0)
                expd = jnp.exp2((scores - highest) * log2e8)
                share = jnp.where(same_cell, 1.0 / jnp.sum(expd, axis=0), 0.0)
                probs = (expd * share).reshape(128, 128).astype(BF16)
                heads.append(jnp.dot(value, probs, preferred_element_type=F32).astype(BF16))
            blocks.append(jnp.concatenate(heads, axis=0))
        attended = jnp.concatenate(blocks, axis=1)
        mixture = residual + jnp.dot(wo[...], attended, preferred_element_type=F32)
        pre_out = halved_silu(mixture * (0.5 * inv_rms(mixture))).astype(BF16)
        taps = jnp.dot(wout[...], pre_out, preferred_element_type=F32)
        for a in range(3):
            accs[r + 2 - a] += taps[16 * a : 16 * a + 16]
    src = iota((256, 128), 0)
    dst = iota((256, 128), 1)
    same_half = src % 128 // 8 % 2 == dst // 64
    spot = 16 * tile + src // 128 * 8 + src % 8 - dst % 64
    pair_of = iota((1, 1, 256), 2) % 128 // 16
    pair_no = iota((8, 1, 256), 0)
    total = None
    for b in range(3):
        chosen = (same_half & (spot == b - 1)).astype(F32).astype(BF16)
        part = jnp.concatenate([accs[:, 4 * b + ch, :] for ch in range(4)], axis=0)
        high = part.astype(BF16).astype(F32)
        for piece in (high, part - high):
            wide = jnp.where(pair_of == pair_no, piece[None], 0.0)
            term = jnp.dot(
                wide.reshape(256, 256).astype(BF16), chosen, preferred_element_type=F32
            )
            total = term if total is None else total + term
    for k, out in enumerate((o0, o1, o2, o3)):
        out[...] = total[64 * k : 64 * k + 64].astype(BF16)


def core(slabs, win, wres, wqkv, wo, wout):
    out = jax.ShapeDtypeStruct((64, 128), BF16)
    vmem = pl.BlockSpec(memory_space=pltpu.VMEM)
    return pl.pallas_call(
        core_kernel,
        out_shape=(out,) * 4,
        in_specs=[vmem] * 9,
        out_specs=(vmem,) * 4,
        scratch_shapes=[
            pltpu.VMEM((7 * 960, 256), BF16),
            pltpu.VMEM((5, 320, 256), F32),
            pltpu.VMEM((8, 16, 256), F32),
        ],
        compiler_params=pltpu.CompilerParams(vmem_limit_bytes=48 * 1024 * 1024),
        cost_estimate=pl.CostEstimate(
            flops=4_000_000_000, bytes_accessed=3_000_000, transcendentals=3_000_000
        ),
    )(*slabs, win, wres, wqkv, wo, wout)


def local(
    latents,
    step_noise,
    fresh_noise,
    timesteps,
    step_coefs,
    inlet_weight,
    time_first,
    time_second,
    res_weight,
    query_weight,
    key_weight,
    value_weight,
    output_weight,
    outlet_weight,
):
    latent = latents[0]
    narrow = latent.astype(BF16)
    below = from_row(narrow[:, :, 3:], 1)
    above = from_row(narrow[:, :, :2], -1)
    embedded = embed_steps(timesteps).astype(BF16)
    hidden = jax.nn.silu(jnp.dot(embedded, time_first, preferred_element_type=F32)).astype(BF16)
    shift = jnp.dot(hidden, time_second, preferred_element_type=F32)
    high = lax.reduce_precision(shift, 8, 7)
    split = jnp.stack([high, shift - high]).reshape(2, 4, 5, 64)
    split = jnp.transpose(split, (2, 1, 0, 3)).reshape(20, 128).astype(BF16)
    split = jnp.pad(split, ((0, 12), (0, 0)))
    rows = jnp.concatenate([below, narrow, above, jnp.zeros_like(narrow[:, :, :1])], axis=2)
    rows = jnp.transpose(rows.reshape(2, 2, 40, 64), (0, 2, 1, 3)).reshape(80, 128)
    slab = jnp.concatenate([rows, split], axis=0)
    slabs = [slab] + [from_partner(slab, k) for k in (1, 2, 3)]
    win = jnp.transpose(inlet_weight.reshape(3, 3, 4, C), (3, 1, 2, 0))
    win = jnp.pad(win, ((0, 0), (0, 0), (0, 0), (0, 7))).reshape(C, 120)
    win = jnp.pad(win, ((0, 0), (0, 8)))
    wres = res_weight.reshape(9 * C, C).T
    wqkv = jnp.concatenate([query_weight, key_weight, value_weight], axis=1).T
    wo = output_weight.T
    wout = jnp.transpose(outlet_weight.reshape(3, 3, C, 4), (0, 1, 3, 2)).reshape(3, 12, C)
    wout = jnp.pad(wout, ((0, 0), (0, 4), (0, 0))).reshape(48, C)
    sent = core(slabs, win, wres, wqkv, wo, wout)
    total = sent[0].astype(F32)
    for k in (1, 2, 3):
        total = total + from_partner(sent[k], k).astype(F32)
    total = total.reshape(2, 4, 8, 128)
    from_below = from_row(total[:, :, 6], 1)
    from_above = from_row(total[:, :, 0], -1)
    middle = total[:, :, 1:6]
    middle = middle + jnp.pad(
        from_below[:, :, None], ((0, 0), (0, 0), (0, 4), (0, 0))
    ) + jnp.pad(from_above[:, :, None], ((0, 0), (0, 0), (4, 0), (0, 0)))
    predicted = jnp.transpose(middle.reshape(2, 4, 5, 2, 64), (0, 3, 1, 2, 4)).reshape(4, 4, 5, 64)

    def per_slot(i):
        return step_coefs[i][:, None, None, None]

    stepped = per_slot(0) * latent + per_slot(1) * predicted + per_slot(2) * step_noise[0]
    count = lax.axis_size("chain")
    arrived = lax.ppermute(stepped[:1], "chain", [(i + 1, i) for i in range(count - 1)])
    is_last = lax.axis_index("chain") == count - 1
    tail = jnp.where(is_last, fresh_noise, arrived)
    advanced = jnp.concatenate([stepped[1:], tail], axis=0)
    return stepped[None], advanced[None]


def solution(mesh):
    rows = P(None, "chain", None, "mp", None)
    return jax.shard_map(
        local,
        mesh=mesh,
        in_specs=(rows, rows, P(None, None, "mp", None), P("chain"), P(None, "chain"))
        + (P(),) * 9,
        out_specs=(rows, rows),
        check_vma=False,
    )
```

```python
import functools
import math

import jax
import jax.numpy as jnp
from jax import lax
from jax.experimental import pallas as pl
from jax.experimental.pallas import tpu as pltpu
from jax.sharding import PartitionSpec as P

F32 = jnp.float32
BF16 = jnp.bfloat16
HEADS = 5
HEAD_DIM = 64
C = 320
ROWS = 5
GROUP = 4


def from_partner(block, bits):
    count = lax.axis_size("chain")
    return lax.ppermute(block, "chain", [(i, i ^ bits) for i in range(count)])


def from_row(block, by):
    count = lax.axis_size("mp")
    return lax.ppermute(block, "mp", [(i, (i + by) % count) for i in range(count)])


def embed_steps(timesteps):
    half_dim = C // 2
    frequency = jnp.exp(-math.log(10000.0) * jnp.arange(half_dim, dtype=F32) / half_dim)
    angles = timesteps.astype(F32)[:, None] * frequency[None, :]
    return jnp.concatenate([jnp.cos(angles), jnp.sin(angles)], axis=1)


def halved_silu(half):
    return half * jnp.tanh(half) + half


def inv_rms(values):
    return lax.rsqrt(jnp.sum(values * values, axis=0, keepdims=True) * (1.0 / C) + 1e-05)


def iota(shape, dim):
    return lax.broadcasted_iota(jnp.int32, shape, dim)


def mm(a, b):
    return jnp.dot(a, b, preferred_element_type=F32)


def prep_kernel(inlet, wres, outlet, win_t, wres_t, wout_t, rows):
    rows[...] = jnp.zeros_like(rows)
    for dy in range(3):
        for dx in range(3):
            at = 32 * dx + 4 * dy
            rows[at : at + 4, :] = inlet[3 * dy + dx].astype(F32)
    taps = rows[...].T
    for r in range(6):
        win_t[r] = (taps if r == 0 else pltpu.roll(taps, 4 * r, 1)).astype(BF16)
    for at in range(0, 9 * C, 128):
        size = min(128, 9 * C - at)
        wres_t[:, at : at + size] = wres[at : at + size, :].T
    for a in range(3):
        for b in range(3):
            at = 16 * a + 4 * b
            rows[at : at + 4, :] = outlet[3 * a + b].astype(F32)
        rows[16 * a + 12 : 16 * a + 16, :] = jnp.zeros((4, C), F32)
    wout_t[...] = rows[:48, :].astype(BF16)


def prep(inlet, wres, outlet):
    vmem = pl.BlockSpec(memory_space=pltpu.VMEM)
    shapes = ((6, C, 128), (C, 9 * C), (48, C))
    return pl.pallas_call(
        prep_kernel,
        out_shape=tuple(jax.ShapeDtypeStruct(s, BF16) for s in shapes),
        in_specs=[vmem] * 3,
        out_specs=(vmem,) * 3,
        scratch_shapes=[pltpu.VMEM((128, C), F32)],
        compiler_params=pltpu.CompilerParams(vmem_limit_bytes=32 * 1024 * 1024),
        cost_estimate=pl.CostEstimate(
            flops=2_000_000_000, bytes_accessed=6_000_000, transcendentals=0
        ),
    )(inlet, wres, outlet)


def core_kernel(
    s0, s1, s2, s3, win, wres, wq, wk, wv, wo_in, wout,
    o0, o1, o2, o3,
    opn, act, res, nrm, qkv, scr, att, accs, wqkv, wo,
):
    tile = lax.axis_index("chain") % GROUP
    row_block = lax.axis_index("mp")
    last_row = lax.axis_size("mp") - 1
    slabs = [s0[...], s1[...], s2[...], s3[...]]
    shift_rows = jnp.concatenate([s[96:128] for s in slabs], axis=0)
    er, el = iota((128, 640), 0), iota((128, 640), 1)
    pick = (er % 32 // 4 == el // 128) & (er // 32 * 4 + er % 4 == el % 128 // 8)
    spread = mm(shift_rows.astype(F32).T.astype(BF16), pick.astype(F32).astype(BF16))
    spread = spread[:64] + spread[64:]
    shift = jnp.concatenate([spread[:, 128 * i : 128 * i + 128] for i in range(5)], axis=0) * 0.5
    latent = jnp.concatenate([s[:96] for s in slabs], axis=0)
    lane = iota((128, 384), 1)
    cell, slot, block = lane % 8, lane % 128 // 8, lane // 128
    at = jnp.where(
        block < 2,
        16 * tile + 8 * block + cell,
        jnp.where(cell == 0, 16 * tile - 1, jnp.where(cell == 7, 16 * tile + 16, -1000)),
    )
    src = iota((128, 384), 0)
    same_half = src // 64 == slot % 2
    pair_of = iota((1, 1, 384), 2) % 128 // 16
    pair_no = iota((8, 1, 384), 0)
    row_of = iota((48, 384), 0) // 4
    inside = ((row_block > 0) | (row_of >= 3)) & ((row_block < last_row) | (row_of < 3 + ROWS))
    columns = []
    for dx in range(3):
        chosen = same_half & (src % 64 == at + (dx - 1))
        moved = mm(latent, chosen.astype(F32).astype(BF16))
        moved = jnp.where(pair_of == pair_no, moved.reshape(8, 48, 384), 0.0)
        columns.append(jnp.where(inside, jnp.sum(moved, axis=0), 0.0))
    empty = jnp.zeros((32, 384), F32)
    upper = jnp.concatenate([c[:32] for c in columns] + [empty], axis=0).astype(BF16)
    lower = jnp.concatenate([c[16:] for c in columns] + [empty], axis=0).astype(BF16)

    lane1 = iota((1, 128), 1)
    cell1 = lane1 % 8
    first, last = cell1 == 0, cell1 == 7
    side = jnp.where(
        first & (tile > 0), 1.0, jnp.where(last & (tile < GROUP - 1), 1.0, 0.0)
    )
    same_cell = iota((8, 128), 0) == iota((8, 128), 1) % 8
    log2e8 = math.log2(math.e) / math.sqrt(HEAD_DIM)

    def open_row(r):
        opn[r] = mm(win[r], upper) if r < 6 else mm(win[r - 4], lower)

    def activate(r):
        opening = opn[r]
        scale = inv_rms(opening) * 0.5
        parts = []
        for t in range(3):
            piece = slice(128 * t, 128 * t + 128)
            part = halved_silu(opening[:, piece] * scale[:, piece] + shift)
            if t == 2:
                part = part * side
            if r < 2:
                part = part * jnp.where(row_block > 0, 1.0, 0.0)
            if r > ROWS + 1:
                part = part * jnp.where(row_block < last_row, 1.0, 0.0)
            parts.append(part)
        a0, a1, edge = parts
        base = 960 * r
        act[base : base + 320, :128] = jnp.where(first, edge, pltpu.roll(a0, 1, 1)).astype(BF16)
        act[base : base + 320, 128:] = jnp.where(
            first, pltpu.roll(a0, 121, 1), pltpu.roll(a1, 1, 1)
        ).astype(BF16)
        act[base + 320 : base + 640, :128] = a0.astype(BF16)
        act[base + 320 : base + 640, 128:] = a1.astype(BF16)
        act[base + 640 : base + 960, :128] = jnp.where(
            last, pltpu.roll(a1, 7, 1), pltpu.roll(a0, 127, 1)
        ).astype(BF16)
        act[base + 640 : base + 960, 128:] = jnp.where(
            last, edge, pltpu.roll(a1, 127, 1)
        ).astype(BF16)

    def convolve(r):
        residual = opn[r + 1, :, :256] + mm(wres[...], act[960 * r : 960 * r + 2880, :])
        res[r] = residual
        nrm[r] = (residual * inv_rms(residual)).astype(BF16)

    def project(r):
        qkv[r] = mm(wqkv[...], nrm[r]).astype(BF16)

    def score(r):
        for b in range(2):
            piece = slice(128 * b, 128 * b + 128)
            for h in range(HEADS):
                scr[r % 2, HEADS * b + h] = lax.dot_general(
                    qkv[r, 320 + 64 * h : 384 + 64 * h, piece],
                    qkv[r, 64 * h : 64 * h + 64, piece],
                    (((0,), (0,)), ((), ())),
                    preferred_element_type=F32,
                ).reshape(16, 8, 128)

    def attend(r):
        probs = []
        for i in range(2 * HEADS):
            scores = scr[r % 2, i]
            highest = jnp.max(scores, axis=0)
            expd = jnp.exp2((scores - highest) * log2e8)
            share = jnp.where(same_cell, 1.0 / jnp.sum(expd, axis=0), 0.0)
            probs.append((expd * share).reshape(128, 128).astype(BF16))
        for b in range(2):
            piece = slice(128 * b, 128 * b + 128)
            for h in range(HEADS):
                value = qkv[r, 640 + 64 * h : 704 + 64 * h, piece]
                att[r, 64 * h : 64 * h + 64, piece] = mm(value, probs[HEADS * b + h]).astype(BF16)

    def mix(r):
        mixture = res[r] + mm(wo[...], att[r])
        outer = halved_silu(mixture * (0.5 * inv_rms(mixture)))
        if r == 0:
            outer = outer * jnp.where(row_block > 0, 1.0, 0.0)
        if r == ROWS + 1:
            outer = outer * jnp.where(row_block < last_row, 1.0, 0.0)
        nrm[r] = outer.astype(BF16)

    def outlet(r):
        taps = mm(wout[...], nrm[r])
        for a in range(3):
            if 0 <= r - a < ROWS:
                accs[r - a] += taps[16 * a : 16 * a + 16]

    accs[...] = jnp.zeros_like(accs)
    for i, w in enumerate((wq, wk, wv)):
        wqkv[C * i : C * i + C, :] = w[...].T
    wo[...] = wo_in[...].T
    count = ROWS + 2
    for r in range(count + 2):
        open_row(r)
    for r in range(3):
        activate(r)
    for step in range(count + 5):
        if step < count:
            convolve(step)
            if step < count - 1:
                activate(step + 3)
        for late, stage in enumerate((project, score, attend, mix, outlet), 1):
            if 0 <= step - late < count:
                stage(step - late)
    src = iota((256, 128), 0)
    dst = iota((256, 128), 1)
    same_half = src % 128 // 8 % 2 == dst // 64
    spot = 16 * tile + src // 128 * 8 + src % 8 - dst % 64
    pair_of = iota((1, 1, 256), 2) % 128 // 16
    pair_no = iota((8, 1, 256), 0)
    total = None
    for b in range(3):
        chosen = (same_half & (spot == b - 1)).astype(F32).astype(BF16)
        part = accs[:, 4 * b : 4 * b + 4, :].reshape(24, 256)
        high = part.astype(BF16).astype(F32)
        for piece in (high, part - high):
            wide = jnp.where(pair_of == pair_no, piece[None], 0.0)
            term = mm(wide.reshape(192, 256).astype(BF16), chosen)
            total = term if total is None else total + term
    for k, out in enumerate((o0, o1, o2, o3)):
        out[...] = total[48 * k : 48 * k + 48].astype(BF16)


def core(slabs, win, wres, wq, wk, wv, wo, wout):
    out = jax.ShapeDtypeStruct((48, 128), BF16)
    vmem = pl.BlockSpec(memory_space=pltpu.VMEM)
    return pl.pallas_call(
        core_kernel,
        out_shape=(out,) * 4,
        in_specs=[vmem] * 11,
        out_specs=(vmem,) * 4,
        scratch_shapes=[
            pltpu.VMEM((ROWS + 4, C, 384), F32),
            pltpu.VMEM(((ROWS + 4) * 960, 256), BF16),
            pltpu.VMEM((ROWS + 2, C, 256), F32),
            pltpu.VMEM((ROWS + 2, C, 256), BF16),
            pltpu.VMEM((ROWS + 2, 3 * C, 256), BF16),
            pltpu.VMEM((2, 10, 16, 8, 128), F32),
            pltpu.VMEM((ROWS + 2, C, 256), BF16),
            pltpu.VMEM((ROWS + 1, 16, 256), F32),
            pltpu.VMEM((3 * C, C), BF16),
            pltpu.VMEM((C, C), BF16),
        ],
        compiler_params=pltpu.CompilerParams(vmem_limit_bytes=36 * 1024 * 1024),
        cost_estimate=pl.CostEstimate(
            flops=4_000_000_000, bytes_accessed=3_000_000, transcendentals=3_000_000
        ),
    )(*slabs, win, wres, wq, wk, wv, wo, wout)


def local(
    latents,
    step_noise,
    fresh_noise,
    timesteps,
    step_coefs,
    inlet_weight,
    time_first,
    time_second,
    res_weight,
    query_weight,
    key_weight,
    value_weight,
    output_weight,
    outlet_weight,
):
    latent = jnp.transpose(latents[0], (0, 2, 1, 3))
    noise = jnp.transpose(step_noise[0], (0, 2, 1, 3))
    fresh = jnp.transpose(fresh_noise, (0, 2, 1, 3))
    below = from_row(latent, 1)[:, ROWS - 3 :]
    above = from_row(latent, -1)[:, :3]
    embedded = embed_steps(timesteps).astype(BF16)
    hidden = jax.nn.silu(jnp.dot(embedded, time_first, preferred_element_type=F32)).astype(BF16)
    shift = jnp.dot(hidden, time_second, preferred_element_type=F32)
    high = lax.reduce_precision(shift, 8, 7)
    split = jnp.stack([high, shift - high]).reshape(2, 4, 5, 64)
    split = jnp.transpose(split, (2, 1, 0, 3)).reshape(20, 128).astype(BF16)
    split = jnp.pad(split, ((0, 12), (0, 0)))
    rows = jnp.concatenate([below, latent, above, jnp.zeros_like(latent[:, :1])], axis=1)
    rows = jnp.transpose(rows.reshape(2, 2, 48, 64), (0, 2, 1, 3)).reshape(96, 128).astype(BF16)
    slab = jnp.concatenate([rows, split], axis=0)
    slabs = [slab] + [from_partner(slab, k) for k in (1, 2, 3)]
    win, wres, wout = prep(
        inlet_weight, res_weight.reshape(9 * C, C), jnp.transpose(outlet_weight, (0, 2, 1))
    )
    squares = (query_weight, key_weight, value_weight, output_weight)
    sent = core(slabs, win, wres, *squares, wout)
    total = sent[0].astype(F32)
    for k in (1, 2, 3):
        total = total + from_partner(sent[k], k).astype(F32)
    middle = total.reshape(2, 6, 4, 128)[:, :ROWS]
    predicted = jnp.transpose(middle.reshape(2, 5, 4, 2, 64), (0, 3, 1, 2, 4)).reshape(4, 5, 4, 64)

    def per_slot(i):
        return step_coefs[i][:, None, None, None]

    stepped = per_slot(0) * latent + per_slot(1) * predicted + per_slot(2) * noise
    count = lax.axis_size("chain")
    arrived = lax.ppermute(stepped[:1], "chain", [(i, (i - 1) % count) for i in range(count)])
    is_last = lax.axis_index("chain") == count - 1
    tail = jnp.where(is_last, fresh, arrived)
    advanced = jnp.concatenate([stepped[1:], tail], axis=0)
    return tuple(jnp.transpose(x, (0, 2, 1, 3))[None] for x in (stepped, advanced))


def solution(mesh):
    rows = P(None, "chain", None, "mp", None)
    return jax.shard_map(
        local,
        mesh=mesh,
        in_specs=(rows, rows, P(None, None, "mp", None), P("chain"), P(None, "chain"))
        + (P(),) * 9,
        out_specs=(rows, rows),
        check_vma=False,
    )
```

```python
import functools
import math

import jax
import jax.numpy as jnp
from jax import lax
from jax.experimental import pallas as pl
from jax.experimental.pallas import tpu as pltpu
from jax.sharding import PartitionSpec as P

F32 = jnp.float32
BF16 = jnp.bfloat16
HEADS = 5
HEAD_DIM = 64
C = 320
ROWS = 5
GROUP = 4


def from_partner(block, bits):
    count = lax.axis_size("chain")
    return lax.ppermute(block, "chain", [(i, i ^ bits) for i in range(count)])


def from_row(block, by):
    count = lax.axis_size("mp")
    return lax.ppermute(block, "mp", [(i, (i + by) % count) for i in range(count)])


def embed_steps(timesteps):
    half_dim = C // 2
    frequency = jnp.exp(-math.log(10000.0) * jnp.arange(half_dim, dtype=F32) / half_dim)
    angles = timesteps.astype(F32)[:, None] * frequency[None, :]
    return jnp.concatenate([jnp.cos(angles), jnp.sin(angles)], axis=1)


def halved_silu(half):
    return half * jnp.tanh(half) + half


def inv_rms(values):
    return lax.rsqrt(jnp.sum(values * values, axis=0, keepdims=True) * (1.0 / C) + 1e-05)


def iota(shape, dim):
    return lax.broadcasted_iota(jnp.int32, shape, dim)


def select(where, a, b):
    return jnp.where(jnp.broadcast_to(where, a.shape), a, b)


def mm(a, b):
    return jnp.dot(a, b, preferred_element_type=F32)


def prep_kernel(inlet, wres, outlet, win_t, wres_t, wout_t, gather, pick, scatter, rows):
    tile = lax.axis_index("chain") % GROUP
    lane = iota((128, 384), 1)
    cell, slot, block = lane % 8, lane % 128 // 8, lane // 128
    at = jnp.where(
        block < 2,
        16 * tile + 8 * block + cell,
        jnp.where(cell == 0, 16 * tile - 1, jnp.where(cell == 7, 16 * tile + 16, -1000)),
    )
    src = iota((128, 384), 0)
    same_half = src // 64 == slot % 2
    for dx in range(3):
        gather[dx] = (same_half & (src % 64 == at + (dx - 1))).astype(F32).astype(BF16)
    er, el = iota((128, 640), 0), iota((128, 640), 1)
    spot = (er % 32 // 4 == el // 128) & (er // 32 * 4 + er % 4 == el % 128 // 8)
    pick[...] = spot.astype(F32).astype(BF16)
    src, dst = iota((256, 128), 0), iota((256, 128), 1)
    same_half = src % 128 // 8 % 2 == dst // 64
    spot = 16 * tile + src // 128 * 8 + src % 8 - dst % 64
    for b in range(3):
        scatter[b] = (same_half & (spot == b - 1)).astype(F32).astype(BF16)
    rows[...] = jnp.zeros_like(rows)
    for dy in range(3):
        for dx in range(3):
            at = 32 * dx + 4 * dy
            rows[at : at + 4, :] = inlet[3 * dy + dx].astype(F32)
    taps = rows[...].T
    for r in range(6):
        win_t[r] = (taps if r == 0 else pltpu.roll(taps, 4 * r, 1)).astype(BF16)
    for at in range(0, 9 * C, 128):
        size = min(128, 9 * C - at)
        wres_t[:, at : at + size] = wres[at : at + size, :].T
    for a in range(3):
        for b in range(3):
            at = 16 * a + 4 * b
            rows[at : at + 4, :] = outlet[3 * a + b].astype(F32)
        rows[16 * a + 12 : 16 * a + 16, :] = jnp.zeros((4, C), F32)
    wout_t[...] = rows[:48, :].astype(BF16)


def prep(inlet, wres, outlet):
    vmem = pl.BlockSpec(memory_space=pltpu.VMEM)
    shapes = ((6, C, 128), (C, 9 * C), (48, C), (3, 128, 384), (128, 640), (3, 256, 128))
    return pl.pallas_call(
        prep_kernel,
        out_shape=tuple(jax.ShapeDtypeStruct(s, BF16) for s in shapes),
        in_specs=[vmem] * 3,
        out_specs=(vmem,) * 6,
        scratch_shapes=[pltpu.VMEM((128, C), F32)],
        compiler_params=pltpu.CompilerParams(vmem_limit_bytes=32 * 1024 * 1024),
        cost_estimate=pl.CostEstimate(
            flops=2_000_000_000, bytes_accessed=6_000_000, transcendentals=0
        ),
    )(inlet, wres, outlet)


def core_kernel(
    s0, s1, s2, s3, win, wres, wq, wk, wv, wo_in, wout, gather, pick, scatter,
    o0, o1, o2, o3,
    opn, act, res, nrm, qkv, scr, att, accs, wqkv, wo, pairs,
):
    tile = lax.axis_index("chain") % GROUP
    row_block = lax.axis_index("mp")
    last_row = lax.axis_size("mp") - 1
    slabs = [s0[...], s1[...], s2[...], s3[...]]
    shift_rows = jnp.concatenate([s[96:128] for s in slabs], axis=0)
    spread = mm(shift_rows.astype(F32).T.astype(BF16), pick[...])
    spread = spread[:64] + spread[64:]
    shift = jnp.concatenate([spread[:, 128 * i : 128 * i + 128] for i in range(5)], axis=0) * 0.5
    latent = jnp.concatenate([s[:96] for s in slabs], axis=0)
    pair_of = iota((1, 1, 384), 2) % 128 // 16
    pair_no = iota((8, 1, 384), 0)
    row_of = iota((48, 384), 0) // 4
    inside = ((row_block > 0) | (row_of >= 3)) & ((row_block < last_row) | (row_of < 3 + ROWS))
    columns = []
    for dx in range(3):
        moved = mm(latent, gather[dx])
        moved = jnp.where(pair_of == pair_no, moved.reshape(8, 48, 384), 0.0)
        columns.append(jnp.where(inside, jnp.sum(moved, axis=0), 0.0))
    empty = jnp.zeros((32, 384), F32)
    upper = jnp.concatenate([c[:32] for c in columns] + [empty], axis=0).astype(BF16)
    lower = jnp.concatenate([c[16:] for c in columns] + [empty], axis=0).astype(BF16)

    lane1 = iota((1, 128), 1)
    cell1 = lane1 % 8
    first, last = cell1 == 0, cell1 == 7
    side = jnp.where(
        first & (tile > 0), 1.0, jnp.where(last & (tile < GROUP - 1), 1.0, 0.0)
    )
    same_cell = iota((8, 128), 0) == iota((8, 128), 1) % 8
    log2e8 = math.log2(math.e) / math.sqrt(HEAD_DIM)

    def open_row(r):
        opn[r] = mm(win[r], upper) if r < 6 else mm(win[r - 4], lower)

    def activate(r):
        opening = opn[r]
        scale = inv_rms(opening) * 0.5
        parts = []
        for t in range(3):
            piece = slice(128 * t, 128 * t + 128)
            part = halved_silu(opening[:, piece] * scale[:, piece] + shift)
            if t == 2:
                part = part * side
            if r < 2:
                part = part * jnp.where(row_block > 0, 1.0, 0.0)
            if r > ROWS + 1:
                part = part * jnp.where(row_block < last_row, 1.0, 0.0)
            parts.append(part)
        a0, a1, edge = [part.astype(BF16) for part in parts]
        base = 960 * r
        act[base : base + 320, :128] = select(first, edge, pltpu.roll(a0, 1, 1))
        act[base : base + 320, 128:] = select(first, pltpu.roll(a0, 121, 1), pltpu.roll(a1, 1, 1))
        act[base + 320 : base + 640, :128] = a0
        act[base + 320 : base + 640, 128:] = a1
        act[base + 640 : base + 960, :128] = select(
            last, pltpu.roll(a1, 7, 1), pltpu.roll(a0, 127, 1)
        )
        act[base + 640 : base + 960, 128:] = select(last, edge, pltpu.roll(a1, 127, 1))

    def convolve(r):
        residual = opn[r + 1, :, :256] + mm(wres[...], act[960 * r : 960 * r + 2880, :])
        res[r] = residual
        nrm[r] = (residual * inv_rms(residual)).astype(BF16)

    def project(r):
        full = mm(wqkv[...], nrm[r]).astype(BF16)
        qkv[r] = full[C:]
        for b in range(2):
            for h in range(HEADS):
                at = h % 2
                pairs[r % 2, b, h // 2, 64 * at : 64 * at + 64, 128 * at : 128 * at + 128] = full[
                    64 * h : 64 * h + 64, 128 * b : 128 * b + 128
                ]

    def score(r):
        for b in range(2):
            for p in range(3):
                heads = min(2, HEADS - 2 * p)
                wide = lax.dot_general(
                    qkv[r, 128 * p : 128 * p + 64 * heads, 128 * b : 128 * b + 128],
                    pairs[r % 2, b, p, : 64 * heads, : 128 * heads],
                    (((0,), (0,)), ((), ())),
                    preferred_element_type=F32,
                )
                for i in range(heads):
                    part = wide[:, 128 * i : 128 * i + 128]
                    scr[r % 2, HEADS * b + 2 * p + i] = part.reshape(16, 8, 128)

    def attend(r):
        probs = []
        for i in range(2 * HEADS):
            scores = scr[r % 2, i]
            highest = jnp.max(scores, axis=0)
            expd = jnp.exp2((scores - highest) * log2e8)
            share = jnp.where(same_cell, 1.0 / jnp.sum(expd, axis=0), 0.0)
            probs.append((expd * share).reshape(128, 128).astype(BF16))
        for b in range(2):
            piece = slice(128 * b, 128 * b + 128)
            for h in range(HEADS):
                value = qkv[r, C + 64 * h : C + 64 * h + 64, piece]
                att[r, 64 * h : 64 * h + 64, piece] = mm(value, probs[HEADS * b + h]).astype(BF16)

    def mix(r):
        mixture = res[r] + mm(wo[...], att[r])
        outer = halved_silu(mixture * (0.5 * inv_rms(mixture)))
        if r == 0:
            outer = outer * jnp.where(row_block > 0, 1.0, 0.0)
        if r == ROWS + 1:
            outer = outer * jnp.where(row_block < last_row, 1.0, 0.0)
        nrm[r] = outer.astype(BF16)

    def outlet(r):
        taps = mm(wout[...], nrm[r])
        for a in range(3):
            if 0 <= r - a < ROWS:
                accs[r - a] += taps[16 * a : 16 * a + 16]

    accs[...] = jnp.zeros_like(accs)
    pairs[...] = jnp.zeros_like(pairs)
    for i, w in enumerate((wq, wk, wv)):
        wqkv[C * i : C * i + C, :] = w[...].T
    wo[...] = wo_in[...].T
    count = ROWS + 2
    for r in range(4):
        open_row(r)
    for r in range(3):
        activate(r)
    for step in range(count + 5):
        if step < count:
            convolve(step)
            if step < count - 1:
                activate(step + 3)
            if step < count - 2:
                open_row(step + 4)
        for late, stage in enumerate((project, score, attend, mix, outlet), 1):
            if 0 <= step - late < count:
                stage(step - late)
    pair_of = iota((1, 1, 256), 2) % 128 // 16
    pair_no = iota((8, 1, 256), 0)
    total = None
    for b in range(3):
        part = accs[:, 4 * b : 4 * b + 4, :].reshape(24, 256)
        high = part.astype(BF16).astype(F32)
        for piece in (high, part - high):
            wide = jnp.where(pair_of == pair_no, piece[None], 0.0)
            term = mm(wide.reshape(192, 256).astype(BF16), scatter[b])
            total = term if total is None else total + term
    for k, out in enumerate((o0, o1, o2, o3)):
        out[...] = total[48 * k : 48 * k + 48].astype(BF16)


def core(slabs, win, wres, wq, wk, wv, wo, wout, gather, pick, scatter):
    out = jax.ShapeDtypeStruct((48, 128), BF16)
    vmem = pl.BlockSpec(memory_space=pltpu.VMEM)
    return pl.pallas_call(
        core_kernel,
        out_shape=(out,) * 4,
        in_specs=[vmem] * 14,
        out_specs=(vmem,) * 4,
        scratch_shapes=[
            pltpu.VMEM((ROWS + 4, C, 384), F32),
            pltpu.VMEM(((ROWS + 4) * 960, 256), BF16),
            pltpu.VMEM((ROWS + 2, C, 256), F32),
            pltpu.VMEM((ROWS + 2, C, 256), BF16),
            pltpu.VMEM((ROWS + 2, 2 * C, 256), BF16),
            pltpu.VMEM((2, 10, 16, 8, 128), F32),
            pltpu.VMEM((ROWS + 2, C, 256), BF16),
            pltpu.VMEM((ROWS + 1, 16, 256), F32),
            pltpu.VMEM((3 * C, C), BF16),
            pltpu.VMEM((C, C), BF16),
            pltpu.VMEM((2, 2, 3, 128, 256), BF16),
        ],
        compiler_params=pltpu.CompilerParams(vmem_limit_bytes=36 * 1024 * 1024),
        cost_estimate=pl.CostEstimate(
            flops=4_000_000_000, bytes_accessed=3_000_000, transcendentals=3_000_000
        ),
    )(*slabs, win, wres, wq, wk, wv, wo, wout, gather, pick, scatter)


def local(
    latents,
    step_noise,
    fresh_noise,
    timesteps,
    step_coefs,
    inlet_weight,
    time_first,
    time_second,
    res_weight,
    query_weight,
    key_weight,
    value_weight,
    output_weight,
    outlet_weight,
):
    latent = jnp.transpose(latents[0], (0, 2, 1, 3))
    noise = jnp.transpose(step_noise[0], (0, 2, 1, 3))
    fresh = jnp.transpose(fresh_noise, (0, 2, 1, 3))
    narrow = lax.optimization_barrier(latent.astype(BF16))
    below = from_row(narrow, 1)[:, ROWS - 3 :]
    above = from_row(narrow, -1)[:, :3]
    embedded = embed_steps(timesteps).astype(BF16)
    hidden = jax.nn.silu(jnp.dot(embedded, time_first, preferred_element_type=F32)).astype(BF16)
    shift = jnp.dot(hidden, time_second, preferred_element_type=F32)
    high = lax.reduce_precision(shift, 8, 7)
    split = jnp.stack([high, shift - high]).reshape(2, 4, 5, 64)
    split = jnp.transpose(split, (2, 1, 0, 3)).reshape(20, 128).astype(BF16)
    split = jnp.pad(split, ((0, 12), (0, 0)))
    rows = jnp.concatenate([below, narrow, above, jnp.zeros_like(narrow[:, :1])], axis=1)
    rows = jnp.transpose(rows.reshape(2, 2, 48, 64), (0, 2, 1, 3)).reshape(96, 128)
    slab = jnp.concatenate([rows, split], axis=0)
    far, across, near = [from_partner(slab, k) for k in (3, 2, 1)]
    slabs = (slab, near, across, far)
    win, wres, wout, *moves = prep(
        inlet_weight, res_weight.reshape(9 * C, C), jnp.transpose(outlet_weight, (0, 2, 1))
    )
    squares = (query_weight, key_weight, value_weight, output_weight)
    sent = core(slabs, win, wres, *squares, wout, *moves)
    total = sent[0].astype(F32)
    arrived = [from_partner(sent[k], k) for k in (3, 2, 1)]
    for part in arrived:
        total = total + part.astype(F32)
    middle = total.reshape(2, 6, 4, 128)[:, :ROWS]
    predicted = jnp.transpose(middle.reshape(2, 5, 4, 2, 64), (0, 3, 1, 2, 4)).reshape(4, 5, 4, 64)

    def per_slot(i):
        return step_coefs[i][:, None, None, None]

    stepped = per_slot(0) * latent + per_slot(1) * predicted + per_slot(2) * noise
    count = lax.axis_size("chain")
    arrived = lax.ppermute(stepped[:1], "chain", [(i, (i - 1) % count) for i in range(count)])
    is_last = lax.axis_index("chain") == count - 1
    tail = jnp.where(is_last, fresh, arrived)
    advanced = jnp.concatenate([stepped[1:], tail], axis=0)
    return tuple(jnp.transpose(x, (0, 2, 1, 3))[None] for x in (stepped, advanced))


def solution(mesh):
    rows = P(None, "chain", None, "mp", None)
    return jax.shard_map(
        local,
        mesh=mesh,
        in_specs=(rows, rows, P(None, None, "mp", None), P("chain"), P(None, "chain"))
        + (P(),) * 9,
        out_specs=(rows, rows),
        check_vma=False,
    )
```

```python
import functools
import math

import jax
import jax.numpy as jnp
from jax import lax
from jax.experimental import pallas as pl
from jax.experimental.pallas import tpu as pltpu
from jax.sharding import PartitionSpec as P

F32 = jnp.float32
BF16 = jnp.bfloat16
HEADS = 5
HEAD_DIM = 64
C = 320
ROWS = 5
GROUP = 4


def from_partner(block, bits):
    count = lax.axis_size("chain")
    return lax.ppermute(block, "chain", [(i, i ^ bits) for i in range(count)])


def from_row(block, by):
    count = lax.axis_size("mp")
    return lax.ppermute(block, "mp", [(i, (i + by) % count) for i in range(count)])


def embed_steps(timesteps):
    half_dim = C // 2
    frequency = jnp.exp(-math.log(10000.0) * jnp.arange(half_dim, dtype=F32) / half_dim)
    angles = timesteps.astype(F32)[:, None] * frequency[None, :]
    return jnp.concatenate([jnp.cos(angles), jnp.sin(angles)], axis=1)


def halved_silu(half):
    return half * jnp.tanh(half) + half


def inv_rms(values):
    return lax.rsqrt(jnp.sum(values * values, axis=0, keepdims=True) * (1.0 / C) + 1e-05)


def iota(shape, dim):
    return lax.broadcasted_iota(jnp.int32, shape, dim)


def select(where, a, b):
    return jnp.where(jnp.broadcast_to(where, a.shape), a, b)


def mm(a, b):
    return jnp.dot(a, b, preferred_element_type=F32)


def prep_kernel(inlet, wres, outlet, win_t, wres_t, wout_t, gather, pick, scatter, rows):
    tile = lax.axis_index("chain") % GROUP
    lane = iota((128, 384), 1)
    cell, slot, block = lane % 8, lane % 128 // 8, lane // 128
    at = jnp.where(
        block < 2,
        16 * tile + 8 * block + cell,
        jnp.where(cell == 0, 16 * tile - 1, jnp.where(cell == 7, 16 * tile + 16, -1000)),
    )
    src = iota((128, 384), 0)
    same_half = src // 64 == slot % 2
    for dx in range(3):
        gather[dx] = (same_half & (src % 64 == at + (dx - 1))).astype(F32).astype(BF16)
    er, el = iota((128, 640), 0), iota((128, 640), 1)
    spot = (er % 32 // 4 == el // 128) & (er // 32 * 4 + er % 4 == el % 128 // 8)
    pick[...] = spot.astype(F32).astype(BF16)
    src, dst = iota((256, 128), 0), iota((256, 128), 1)
    same_half = src % 128 // 8 % 2 == dst // 64
    spot = 16 * tile + src // 128 * 8 + src % 8 - dst % 64
    for b in range(3):
        scatter[b] = (same_half & (spot == b - 1)).astype(F32).astype(BF16)
    rows[...] = jnp.zeros_like(rows)
    for dy in range(3):
        for dx in range(3):
            at = 32 * dx + 4 * dy
            rows[at : at + 4, :] = inlet[3 * dy + dx].astype(F32)
    taps = rows[...].T
    for r in range(6):
        win_t[r] = (taps if r == 0 else pltpu.roll(taps, 4 * r, 1)).astype(BF16)
    for at in range(0, 9 * C, 128):
        size = min(128, 9 * C - at)
        wres_t[:, at : at + size] = wres[at : at + size, :].T
    for a in range(3):
        for b in range(3):
            at = 16 * a + 4 * b
            rows[at : at + 4, :] = outlet[3 * a + b].astype(F32)
        rows[16 * a + 12 : 16 * a + 16, :] = jnp.zeros((4, C), F32)
    wout_t[...] = rows[:48, :].astype(BF16)


def prep(inlet, wres, outlet):
    vmem = pl.BlockSpec(memory_space=pltpu.VMEM)
    shapes = ((6, C, 128), (C, 9 * C), (48, C), (3, 128, 384), (128, 640), (3, 256, 128))
    return pl.pallas_call(
        prep_kernel,
        out_shape=tuple(jax.ShapeDtypeStruct(s, BF16) for s in shapes),
        in_specs=[vmem] * 3,
        out_specs=(vmem,) * 6,
        scratch_shapes=[pltpu.VMEM((128, C), F32)],
        compiler_params=pltpu.CompilerParams(vmem_limit_bytes=32 * 1024 * 1024),
        cost_estimate=pl.CostEstimate(
            flops=2_000_000_000, bytes_accessed=6_000_000, transcendentals=0
        ),
    )(inlet, wres, outlet)


def core_kernel(
    s0, s1, s2, s3, win, wres, wq, wk, wv, wo_in, wout, gather, pick, scatter,
    o0, o1, o2, o3,
    opn, act, res, nrm, qkv, scr, att, accs, wqkv, wo,
):
    tile = lax.axis_index("chain") % GROUP
    row_block = lax.axis_index("mp")
    last_row = lax.axis_size("mp") - 1
    slabs = [s0[...], s1[...], s2[...], s3[...]]
    shift_rows = jnp.concatenate([s[96:128] for s in slabs], axis=0)
    spread = mm(shift_rows.astype(F32).T.astype(BF16), pick[...])
    spread = spread[:64] + spread[64:]
    shift = jnp.concatenate([spread[:, 128 * i : 128 * i + 128] for i in range(5)], axis=0) * 0.5
    latent = jnp.concatenate([s[:96] for s in slabs], axis=0)
    pair_of = iota((1, 1, 384), 2) % 128 // 16
    pair_no = iota((8, 1, 384), 0)
    row_of = iota((48, 384), 0) // 4
    inside = ((row_block > 0) | (row_of >= 3)) & ((row_block < last_row) | (row_of < 3 + ROWS))
    columns = []
    for dx in range(3):
        moved = mm(latent, gather[dx])
        moved = jnp.where(pair_of == pair_no, moved.reshape(8, 48, 384), 0.0)
        columns.append(jnp.where(inside, jnp.sum(moved, axis=0), 0.0))
    empty = jnp.zeros((32, 384), F32)
    upper = jnp.concatenate([c[:32] for c in columns] + [empty], axis=0).astype(BF16)
    lower = jnp.concatenate([c[16:] for c in columns] + [empty], axis=0).astype(BF16)

    lane1 = iota((1, 128), 1)
    cell1 = lane1 % 8
    first, last = cell1 == 0, cell1 == 7
    side = jnp.where(
        first & (tile > 0), 1.0, jnp.where(last & (tile < GROUP - 1), 1.0, 0.0)
    )
    same_cell = iota((8, 128), 0) == iota((8, 128), 1) % 8
    log2e8 = math.log2(math.e) / math.sqrt(HEAD_DIM)

    def open_row(r):
        opn[r] = mm(win[r], upper) if r < 6 else mm(win[r - 4], lower)

    def activate(r):
        opening = opn[r]
        scale = inv_rms(opening) * 0.5
        parts = []
        for t in range(3):
            piece = slice(128 * t, 128 * t + 128)
            part = halved_silu(opening[:, piece] * scale[:, piece] + shift)
            if t == 2:
                part = part * side
            if r < 2:
                part = part * jnp.where(row_block > 0, 1.0, 0.0)
            if r > ROWS + 1:
                part = part * jnp.where(row_block < last_row, 1.0, 0.0)
            parts.append(part)
        a0, a1, edge = [part.astype(BF16) for part in parts]
        base = 960 * r
        act[base : base + 320, :128] = select(first, edge, pltpu.roll(a0, 1, 1))
        act[base : base + 320, 128:] = select(first, pltpu.roll(a0, 121, 1), pltpu.roll(a1, 1, 1))
        act[base + 320 : base + 640, :128] = a0
        act[base + 320 : base + 640, 128:] = a1
        act[base + 640 : base + 960, :128] = select(
            last, pltpu.roll(a1, 7, 1), pltpu.roll(a0, 127, 1)
        )
        act[base + 640 : base + 960, 128:] = select(last, edge, pltpu.roll(a1, 127, 1))

    def convolve(r):
        residual = opn[r + 1, :, :256] + mm(wres[...], act[960 * r : 960 * r + 2880, :])
        res[r] = residual
        nrm[r] = (residual * inv_rms(residual)).astype(BF16)

    def project(r):
        qkv[r] = mm(wqkv[...], nrm[r]).astype(BF16)

    def score(r):
        for b in range(2):
            piece = slice(128 * b, 128 * b + 128)
            for h in range(HEADS):
                scr[r % 2, HEADS * b + h] = lax.dot_general(
                    qkv[r, C + 64 * h : C + 64 * h + 64, piece],
                    qkv[r, 64 * h : 64 * h + 64, piece],
                    (((0,), (0,)), ((), ())),
                    preferred_element_type=F32,
                ).reshape(16, 8, 128)

    def attend(r):
        probs = []
        for i in range(2 * HEADS):
            scores = scr[r % 2, i]
            highest = jnp.max(scores, axis=0)
            expd = jnp.exp2((scores - highest) * log2e8)
            share = jnp.where(same_cell, 1.0 / jnp.sum(expd, axis=0), 0.0)
            probs.append((expd * share).reshape(128, 128).astype(BF16))
        for b in range(2):
            piece = slice(128 * b, 128 * b + 128)
            for h in range(HEADS):
                value = qkv[r, 2 * C + 64 * h : 2 * C + 64 * h + 64, piece]
                att[r, 64 * h : 64 * h + 64, piece] = mm(value, probs[HEADS * b + h]).astype(BF16)

    def mix(r):
        mixture = res[r] + mm(wo[...], att[r])
        outer = halved_silu(mixture * (0.5 * inv_rms(mixture)))
        if r == 0:
            outer = outer * jnp.where(row_block > 0, 1.0, 0.0)
        if r == ROWS + 1:
            outer = outer * jnp.where(row_block < last_row, 1.0, 0.0)
        nrm[r] = outer.astype(BF16)

    def outlet(r):
        taps = mm(wout[...], nrm[r])
        for a in range(3):
            if 0 <= r - a < ROWS:
                accs[r - a] += taps[16 * a : 16 * a + 16]

    accs[...] = jnp.zeros_like(accs)
    for i, w in enumerate((wq, wk, wv)):
        wqkv[C * i : C * i + C, :] = w[...].T
    wo[...] = wo_in[...].T
    count = ROWS + 2
    for r in range(4):
        open_row(r)
    for r in range(3):
        activate(r)
    for step in range(count + 5):
        if step < count:
            convolve(step)
            if step < count - 1:
                activate(step + 3)
            if step < count - 2:
                open_row(step + 4)
        for late, stage in enumerate((project, score, attend, mix, outlet), 1):
            if 0 <= step - late < count:
                stage(step - late)
    pair_of = iota((1, 1, 256), 2) % 128 // 16
    pair_no = iota((8, 1, 256), 0)
    total = None
    for b in range(3):
        part = accs[:, 4 * b : 4 * b + 4, :].reshape(24, 256)
        wide = jnp.where(pair_of == pair_no, part[None], 0.0)
        term = mm(wide.reshape(192, 256).astype(BF16), scatter[b])
        total = term if total is None else total + term
    for k, out in enumerate((o0, o1, o2, o3)):
        out[...] = total[48 * k : 48 * k + 48].astype(BF16)


def core(slabs, win, wres, wq, wk, wv, wo, wout, gather, pick, scatter):
    out = jax.ShapeDtypeStruct((48, 128), BF16)
    vmem = pl.BlockSpec(memory_space=pltpu.VMEM)
    return pl.pallas_call(
        core_kernel,
        out_shape=(out,) * 4,
        in_specs=[vmem] * 14,
        out_specs=(vmem,) * 4,
        scratch_shapes=[
            pltpu.VMEM((ROWS + 4, C, 384), F32),
            pltpu.VMEM(((ROWS + 4) * 960, 256), BF16),
            pltpu.VMEM((ROWS + 2, C, 256), F32),
            pltpu.VMEM((ROWS + 2, C, 256), BF16),
            pltpu.VMEM((ROWS + 2, 3 * C, 256), BF16),
            pltpu.VMEM((2, 10, 16, 8, 128), F32),
            pltpu.VMEM((ROWS + 2, C, 256), BF16),
            pltpu.VMEM((ROWS + 1, 16, 256), F32),
            pltpu.VMEM((3 * C, C), BF16),
            pltpu.VMEM((C, C), BF16),
        ],
        compiler_params=pltpu.CompilerParams(vmem_limit_bytes=36 * 1024 * 1024),
        cost_estimate=pl.CostEstimate(
            flops=4_000_000_000, bytes_accessed=3_000_000, transcendentals=3_000_000
        ),
    )(*slabs, win, wres, wq, wk, wv, wo, wout, gather, pick, scatter)


def local(
    latents,
    step_noise,
    fresh_noise,
    timesteps,
    step_coefs,
    inlet_weight,
    time_first,
    time_second,
    res_weight,
    query_weight,
    key_weight,
    value_weight,
    output_weight,
    outlet_weight,
):
    latent = jnp.transpose(latents[0], (0, 2, 1, 3))
    noise = jnp.transpose(step_noise[0], (0, 2, 1, 3))
    fresh = jnp.transpose(fresh_noise, (0, 2, 1, 3))
    narrow = lax.optimization_barrier(latent.astype(BF16))
    below = from_row(narrow, 1)[:, ROWS - 3 :]
    above = from_row(narrow, -1)[:, :3]
    embedded = embed_steps(timesteps).astype(BF16)
    hidden = jax.nn.silu(jnp.dot(embedded, time_first, preferred_element_type=F32)).astype(BF16)
    shift = jnp.dot(hidden, time_second, preferred_element_type=F32)
    high = lax.reduce_precision(shift, 8, 7)
    split = jnp.stack([high, shift - high]).reshape(2, 4, 5, 64)
    split = jnp.transpose(split, (2, 1, 0, 3)).reshape(20, 128).astype(BF16)
    split = jnp.pad(split, ((0, 12), (0, 0)))
    rows = jnp.concatenate([below, narrow, above, jnp.zeros_like(narrow[:, :1])], axis=1)
    rows = jnp.transpose(rows.reshape(2, 2, 48, 64), (0, 2, 1, 3)).reshape(96, 128)
    slab = jnp.concatenate([rows, split], axis=0)
    far, across, near = [from_partner(slab, k) for k in (3, 2, 1)]
    slabs = (slab, near, across, far)
    win, wres, wout, *moves = prep(
        inlet_weight, res_weight.reshape(9 * C, C), jnp.transpose(outlet_weight, (0, 2, 1))
    )
    squares = (query_weight, key_weight, value_weight, output_weight)
    sent = core(slabs, win, wres, *squares, wout, *moves)
    total = sent[0].astype(F32)
    arrived = [from_partner(sent[k], k) for k in (3, 2, 1)]
    for part in arrived:
        total = total + part.astype(F32)
    middle = total.reshape(2, 6, 4, 128)[:, :ROWS]
    predicted = jnp.transpose(middle.reshape(2, 5, 4, 2, 64), (0, 3, 1, 2, 4)).reshape(4, 5, 4, 64)

    def per_slot(i):
        return step_coefs[i][:, None, None, None]

    stepped = per_slot(0) * latent + per_slot(1) * predicted + per_slot(2) * noise
    count = lax.axis_size("chain")
    arrived = lax.ppermute(stepped[:1], "chain", [(i, (i - 1) % count) for i in range(count)])
    is_last = lax.axis_index("chain") == count - 1
    tail = jnp.where(is_last, fresh, arrived)
    advanced = jnp.concatenate([stepped[1:], tail], axis=0)
    return tuple(jnp.transpose(x, (0, 2, 1, 3))[None] for x in (stepped, advanced))


def solution(mesh):
    rows = P(None, "chain", None, "mp", None)
    return jax.shard_map(
        local,
        mesh=mesh,
        in_specs=(rows, rows, P(None, None, "mp", None), P("chain"), P(None, "chain"))
        + (P(),) * 9,
        out_specs=(rows, rows),
        check_vma=False,
    )
```
